512 devices in a mesh: row: 16 (over z), col: 8 (over y, core), rep: 4 (over x).
Axes of the slice: x: 4, y: 4, z: 16, core: 2. Of those that a mesh axis runs over, the one named last changes fastest.
Arguments:
- momentum: bfloat16 [8192, 32768], P('row', ('col', 'rep')), may hold values from -16 to 16
- gradient: bfloat16 [8192, 32768], P('row', ('col', 'rep')), may hold values from -16 to 16
- right_prev: bfloat16 [32768, 256], P(('col', 'rep')), may hold values from -0.03125 to 0.03125
Outputs:
- momentum_next: bfloat16 [8192, 32768], P('row', ('col', 'rep'))
- left_factor: float32 [8192, 256], P('row')
- right_factor: float32 [32768, 256], P(('col', 'rep'))
The draws below stay inside these ranges and needn't reach their ends.
All inputs are finite; a program needn't handle non-finite values.
Results may differ from the reference program's by a relative error of at most 0.013.
Values may be sent and summed in bfloat16 or wider, within the bound.
No kernel may reach another device: no remote copies, remote signals or barrier semaphores. Data moves between devices by JAX's collectives and lax.ppermute only.
A program may use at most 64 MiB of HBM per device.

```python
import math
import jax
import jax.numpy as jnp
from jax import lax

ROWS = 8192
COLS = 32768
RANK = 256


def shared_structure(key, level_low, level_high):
    count = max(RANK // 8, 2)
    left_key, right_key = jax.random.split(key)
    level_key = jax.random.fold_in(key, 5)
    left_signs = (2 * jax.random.randint(left_key, (ROWS, count), 0, 2) - 1).astype(jnp.float32)
    right_signs = (2 * jax.random.randint(right_key, (COLS, count), 0, 2) - 1).astype(jnp.float32)
    weight_list = [0.5 ** (4 * index // count) for index in range(count)]
    scaling = 1.0 / math.sqrt(sum((value * value for value in weight_list)))
    weights = jnp.asarray(weight_list, dtype=jnp.float32)
    summed = jnp.dot(left_signs * weights, right_signs.T, precision=lax.Precision.HIGHEST, preferred_element_type=jnp.float32)
    block_levels = jnp.exp(jax.random.uniform(level_key, (32,), jnp.float32, level_low, level_high))
    column_levels = jnp.broadcast_to(block_levels[:, None], (32, COLS // 32)).reshape(COLS)
    return (summed * scaling, column_levels)


def noisy_field(key, amount, structure, column_levels):
    noise = jax.random.normal(key, (ROWS, COLS), jnp.float32)
    field = (noise + amount * structure) * column_levels[None, :]
    return jnp.clip(field, -16.0, 16.0).astype(jnp.bfloat16)


def draw_momentum(key, part):
    structure, column_levels = shared_structure(key, -1.6, 0.7)
    key = jax.random.fold_in(key, 11)
    return noisy_field(key, 2.0, structure, column_levels)


def draw_gradient(key, part):
    structure, column_levels = shared_structure(key, -1.6, 0.7)
    key = jax.random.fold_in(key, 12)
    return noisy_field(key, 0.5, structure, column_levels)


def levels(rng, extent, pieces, least, top_value):
    level = 1.0
    for dim, parts in pieces:
        steps = jax.random.uniform(jax.random.fold_in(jax.random.fold_in(rng, 6), dim), (parts,), jnp.float32, least / len(pieces), top_value / len(pieces))
        level = level * jnp.repeat(jnp.exp(steps), extent[dim] // parts).reshape((-1,) + (1,) * (len(extent) - 1 - dim))
    return level


def centred(own_key, shape, scale, reach, cuts=(), kind=jnp.bfloat16):
    result = scale * jax.random.normal(own_key, shape, jnp.float32)
    if cuts:
        result = result * levels(own_key, shape, cuts, -0.22, 0.18)
    return jnp.clip(result, -reach, reach).astype(kind)


def setup_inputs(seed: int = 0) -> dict:
    arg_keys = jax.random.split(jax.random.key(seed), 4)
    momentum = draw_momentum(jax.random.fold_in(arg_keys[3], 71), 0)
    gradient = draw_gradient(jax.random.fold_in(arg_keys[3], 71), 0)
    right_prev = centred(arg_keys[2], (COLS, RANK), COLS ** -0.5, 0.03125, ((0, 32),))
    return dict(momentum=momentum, gradient=gradient, right_prev=right_prev)


def reference(momentum, gradient, right_prev):
    buffer = (momentum.astype(jnp.float32) + gradient.astype(jnp.float32)).astype(jnp.bfloat16)
    left_raw = jnp.dot(buffer.astype(jnp.float32), right_prev.astype(jnp.float32), preferred_element_type=jnp.float32)
    gram_matrix = jnp.dot(left_raw.T.astype(jnp.float32), left_raw.astype(jnp.float32), precision=lax.Precision.HIGHEST, preferred_element_type=jnp.float32)
    factor = jnp.linalg.cholesky(gram_matrix)
    left_factor = jax.scipy.linalg.solve_triangular(factor, left_raw.T, lower=True).T
    left_low = left_factor.astype(jnp.bfloat16)
    right_low = lax.dot_general(buffer.astype(jnp.float32), left_low.astype(jnp.float32), (((0,), (0,)), ((), ())), preferred_element_type=jnp.float32).astype(jnp.bfloat16)
    outer = lax.dot_general(left_low.astype(jnp.float32), right_low.astype(jnp.float32), (((1,), (1,)), ((), ())), preferred_element_type=jnp.float32)
    momentum_next = (buffer.astype(jnp.float32) - 0.1 * outer).astype(jnp.bfloat16)
    right_wide = right_low.astype(jnp.float32)
    column_sums = lax.optimization_barrier(jnp.sum(right_wide * right_wide, axis=0))
    right_factor = right_wide / (jnp.sqrt(column_sums) + 1e-08)
    return (momentum_next, left_factor, right_factor)
```

```python
import jax
import jax.numpy as jnp
from jax import lax
from jax.experimental import pallas as pl
from jax.experimental.pallas import tpu as pltpu
from jax.sharding import PartitionSpec as P

RANK = 256
BLOCK = 64
WIDE = ("col", "rep")


def dot32(a, b, a_dim, b_dim):
    return lax.dot_general(
        a,
        b,
        (((a_dim,), (b_dim,)), ((), ())),
        precision=lax.Precision.HIGHEST,
        preferred_element_type=jnp.float32,
    )


def eliminate(rows, offset, sub):
    count = len(rows)
    done = []
    for group in range(count):
        first = offset + 8 * group
        cols = [
            [
                jnp.broadcast_to(rows[r][:, first + k : first + k + 1], (8, 128))
                for k in range(8)
            ]
            for r in range(group, count)
        ]
        scale = jnp.zeros((8, 128), jnp.float32)
        for k in range(8):
            pivot = jnp.broadcast_to(cols[0][k][k : k + 1, :], (8, 128))
            inverse = 1.0 / pivot
            scale = jnp.where(sub == k, lax.rsqrt(pivot), scale)
            pivot_row = jnp.broadcast_to(rows[group][k : k + 1, :], (8, 128)) * inverse
            pivot_cols = [
                jnp.broadcast_to(cols[0][j][k : k + 1, :], (8, 128)) * inverse
                for j in range(k + 1, 8)
            ]
            for r in range(group, count):
                factor = cols[r - group][k]
                if r == group:
                    if k == 7:
                        continue
                    factor = jnp.where(sub > k, factor, 0.0)
                rows[r] = rows[r] - factor * pivot_row
                for j in range(k + 1, 8):
                    cols[r - group][j] = cols[r - group][j] - factor * pivot_cols[j - k - 1]
        done.append(rows[group] * scale)
    return done


def inverse_factor_kernel(gram_ref, out_ref, rest_ref):
    sub = lax.broadcasted_iota(jnp.int32, (8, 128), 0)
    lane = lax.broadcasted_iota(jnp.int32, (8, 128), 1)
    rest_ref[...] = gram_ref[...]
    out_ref[...] = jnp.zeros((RANK, RANK), jnp.float32)
    for low in range(0, RANK, BLOCK):
        high = low + BLOCK
        base = low // 128 * 128
        offset = low - base
        other = BLOCK - offset
        rows = []
        for r in range(BLOCK // 8):
            held = rest_ref[low + 8 * r : low + 8 * r + 8, base : base + 128]
            unit = jnp.where(lane == other + 8 * r + sub, 1.0, 0.0)
            rows.append(jnp.where((lane >= offset) & (lane < offset + BLOCK), held, unit))
        block = jnp.concatenate(eliminate(rows, offset, sub), axis=0)
        inverse = block[:, other : other + BLOCK]
        if low:
            out_ref[low:high, 0:low] = dot32(inverse, out_ref[low:high, 0:low], 1, 0)
        out_ref[low:high, low:high] = inverse
        if high < RANK:
            upper = dot32(inverse, rest_ref[low:high, high:RANK], 1, 0)
            solved = out_ref[low:high, 0:high]
            rest_ref[high:RANK, high:RANK] = rest_ref[high:RANK, high:RANK] - dot32(
                upper, upper, 0, 0
            )
            out_ref[high:RANK, 0:high] = out_ref[high:RANK, 0:high] - dot32(upper, solved, 0, 0)


def inverse_factor(gram_matrix):
    return pl.pallas_call(
        inverse_factor_kernel,
        out_shape=jax.ShapeDtypeStruct((RANK, RANK), jnp.float32),
        in_specs=[pl.BlockSpec(memory_space=pltpu.VMEM)],
        out_specs=pl.BlockSpec(memory_space=pltpu.VMEM),
        scratch_shapes=[pltpu.VMEM((RANK, RANK), jnp.float32)],
        cost_estimate=pl.CostEstimate(flops=400_000_000, bytes_accessed=524288, transcendentals=0),
        name="inverse_factor",
    )(gram_matrix)


def scatter_sum(x, axes, count):
    parts = x.reshape(count, x.shape[0] // count, x.shape[1])
    return jnp.sum(lax.all_to_all(parts, axes, 0, 0, tiled=True), axis=0)


def gather(x, axes, count):
    return lax.all_to_all(
        jnp.broadcast_to(x[None], (count,) + x.shape), axes, 0, 0, tiled=True
    )


def split3(x):
    high = lax.reduce_precision(x, 8, 7)
    rest = x - high
    middle = lax.reduce_precision(rest, 8, 7)
    return [v.astype(jnp.bfloat16) for v in (high, middle, rest - middle)]


def local(wide, tall, momentum, gradient, right_prev):
    place = lax.axis_index(WIDE)
    buffer = (momentum.astype(jnp.float32) + gradient.astype(jnp.float32)).astype(jnp.bfloat16)
    left_partial = jnp.dot(buffer, right_prev, preferred_element_type=jnp.float32)
    rows = left_partial.shape[0]
    left_rows = scatter_sum(left_partial, WIDE, wide)
    left_raw = gather(left_rows, WIDE, wide).reshape(rows, RANK)

    share = RANK // wide
    own = lax.dynamic_slice(left_raw, (0, place * share), (rows, share))
    gram_rows = jnp.sum(gather(dot32(own, left_raw, 0, 0), "row", tall), axis=0)
    gram_matrix = gather(gram_rows, WIDE, wide).reshape(RANK, RANK)
    inverse = inverse_factor(gram_matrix)

    pieces = jnp.concatenate(split3(left_raw), axis=1)
    product = lax.dot_general(
        buffer, pieces, (((0,), (0,)), ((), ())), preferred_element_type=jnp.float32
    )
    wide_partial = product[:, :RANK] + (product[:, RANK : 2 * RANK] + product[:, 2 * RANK :])
    right_raw = scatter_sum(wide_partial, "row", tall)

    left_factor = dot32(left_raw, inverse, 1, 1)
    left_low = left_factor.astype(jnp.bfloat16)
    right_rows = dot32(right_raw, inverse, 1, 1).astype(jnp.bfloat16)
    right_low = gather(right_rows, "row", tall).reshape(buffer.shape[1], RANK)
    right_wide = right_low.astype(jnp.float32)
    own_sums = jnp.sum(right_wide * right_wide, axis=0, keepdims=True)
    column_sums = jnp.sum(gather(own_sums, WIDE, wide), axis=0)
    outer = lax.dot_general(
        left_low, right_low, (((1,), (1,)), ((), ())), preferred_element_type=jnp.float32
    )
    momentum_next = (buffer.astype(jnp.float32) - 0.1 * outer).astype(jnp.bfloat16)
    right_factor = right_wide / (jnp.sqrt(column_sums) + 1e-08)
    return (momentum_next, left_factor, right_factor)


def solution(mesh):
    wide = mesh.shape["col"] * mesh.shape["rep"]
    tall = mesh.shape["row"]
    placed = (P("row", WIDE), P("row", WIDE), P(WIDE, None))

    def run(momentum, gradient, right_prev):
        return local(wide, tall, momentum, gradient, right_prev)

    return jax.shard_map(
        run,
        mesh=mesh,
        in_specs=placed,
        out_specs=(P("row", WIDE), P("row", None), P(WIDE, None)),
        check_vma=False,
    )
```

```python
import jax
import jax.numpy as jnp
from jax import lax
from jax.experimental import pallas as pl
from jax.experimental.pallas import tpu as pltpu
from jax.sharding import PartitionSpec as P

RANK = 256
BLOCK = 64
WIDE = ("col", "rep")


def dot32(a, b, a_dim, b_dim):
    return lax.dot_general(
        a,
        b,
        (((a_dim,), (b_dim,)), ((), ())),
        precision=lax.Precision.HIGHEST,
        preferred_element_type=jnp.float32,
    )


def eliminate(rows, offset, sub):
    count = len(rows)
    done = []
    for group in range(count):
        first = offset + 8 * group
        cols = [
            [
                jnp.broadcast_to(rows[r][:, first + k : first + k + 1], (8, 128))
                for k in range(8)
            ]
            for r in range(group, count)
        ]
        scale = jnp.zeros((8, 128), jnp.float32)
        for k in range(8):
            pivot = jnp.broadcast_to(cols[0][k][k : k + 1, :], (8, 128))
            inverse = 1.0 / pivot
            scale = jnp.where(sub == k, lax.rsqrt(pivot), scale)
            pivot_row = jnp.broadcast_to(rows[group][k : k + 1, :], (8, 128)) * inverse
            pivot_cols = [
                jnp.broadcast_to(cols[0][j][k : k + 1, :], (8, 128)) * inverse
                for j in range(k + 1, 8)
            ]
            for r in range(group, count):
                factor = cols[r - group][k]
                if r == group:
                    if k == 7:
                        continue
                    factor = jnp.where(sub > k, factor, 0.0)
                rows[r] = rows[r] - factor * pivot_row
                for j in range(k + 1, 8):
                    cols[r - group][j] = cols[r - group][j] - factor * pivot_cols[j - k - 1]
        done.append(rows[group] * scale)
    return done


def inverse_factor_kernel(gram_ref, out_ref, rest_ref):
    sub = lax.broadcasted_iota(jnp.int32, (8, 128), 0)
    lane = lax.broadcasted_iota(jnp.int32, (8, 128), 1)
    rest_ref[...] = gram_ref[...]
    out_ref[...] = jnp.zeros((RANK, RANK), jnp.float32)
    for low in range(0, RANK, BLOCK):
        high = low + BLOCK
        base = low // 128 * 128
        offset = low - base
        other = BLOCK - offset
        rows = []
        for r in range(BLOCK // 8):
            held = rest_ref[low + 8 * r : low + 8 * r + 8, base : base + 128]
            unit = jnp.where(lane == other + 8 * r + sub, 1.0, 0.0)
            rows.append(jnp.where((lane >= offset) & (lane < offset + BLOCK), held, unit))
        block = jnp.concatenate(eliminate(rows, offset, sub), axis=0)
        inverse = block[:, other : other + BLOCK]
        if low:
            out_ref[low:high, 0:low] = dot32(inverse, out_ref[low:high, 0:low], 1, 0)
        out_ref[low:high, low:high] = inverse
        if high < RANK:
            upper = dot32(inverse, rest_ref[low:high, high:RANK], 1, 0)
            solved = out_ref[low:high, 0:high]
            rest_ref[high:RANK, high:RANK] = rest_ref[high:RANK, high:RANK] - dot32(
                upper, upper, 0, 0
            )
            out_ref[high:RANK, 0:high] = out_ref[high:RANK, 0:high] - dot32(upper, solved, 0, 0)


def inverse_factor(gram_matrix):
    return pl.pallas_call(
        inverse_factor_kernel,
        out_shape=jax.ShapeDtypeStruct((RANK, RANK), jnp.float32),
        in_specs=[pl.BlockSpec(memory_space=pltpu.VMEM)],
        out_specs=pl.BlockSpec(memory_space=pltpu.VMEM),
        scratch_shapes=[pltpu.VMEM((RANK, RANK), jnp.float32)],
        cost_estimate=pl.CostEstimate(flops=400_000_000, bytes_accessed=524288, transcendentals=0),
        name="inverse_factor",
    )(gram_matrix)


def scatter_sum(x, axes, count):
    parts = x.reshape(count, x.shape[0] // count, x.shape[1])
    return jnp.sum(lax.all_to_all(parts, axes, 0, 0, tiled=True), axis=0)


def gather(x, axes, count):
    return lax.all_to_all(
        jnp.broadcast_to(x[None], (count,) + x.shape), axes, 0, 0, tiled=True
    )


def split3(x):
    high = lax.reduce_precision(x, 8, 7)
    rest = x - high
    middle = lax.reduce_precision(rest, 8, 7)
    return [v.astype(jnp.bfloat16) for v in (high, middle, rest - middle)]


def local(wide, tall, momentum, gradient, right_prev):
    place = lax.axis_index(WIDE)
    buffer = (momentum.astype(jnp.float32) + gradient.astype(jnp.float32)).astype(jnp.bfloat16)
    left_partial = jnp.dot(buffer, right_prev, preferred_element_type=jnp.float32)
    rows = left_partial.shape[0]
    left_rows = scatter_sum(left_partial, WIDE, wide)
    left_raw = gather(left_rows, WIDE, wide).reshape(rows, RANK)

    wide_partial = sum(
        lax.dot_general(
            buffer, piece, (((0,), (0,)), ((), ())), preferred_element_type=jnp.float32
        )
        for piece in split3(left_raw)
    )
    share = RANK // wide
    own = lax.dynamic_slice(left_raw, (0, place * share), (rows, share))
    own, wide_partial = lax.optimization_barrier((own, wide_partial))
    right_raw = lax.psum_scatter(wide_partial, "row", scatter_dimension=0, tiled=True)
    gram_rows = jnp.sum(gather(dot32(own, left_raw, 0, 0), "row", tall), axis=0)
    gram_matrix = gather(gram_rows, WIDE, wide).reshape(RANK, RANK)
    inverse = inverse_factor(gram_matrix)

    left_factor = dot32(left_raw, inverse, 1, 1)
    left_low = left_factor.astype(jnp.bfloat16)
    right_rows = dot32(right_raw, inverse, 1, 1).astype(jnp.bfloat16)
    right_low = lax.all_gather(right_rows, "row", axis=0, tiled=True)
    right_wide = right_low.astype(jnp.float32)
    own_sums = jnp.sum(right_wide * right_wide, axis=0, keepdims=True)
    column_sums = jnp.sum(gather(own_sums, WIDE, wide), axis=0)
    outer = lax.dot_general(
        left_low, right_low, (((1,), (1,)), ((), ())), preferred_element_type=jnp.float32
    )
    momentum_next = (buffer.astype(jnp.float32) - 0.1 * outer).astype(jnp.bfloat16)
    right_factor = right_wide / (jnp.sqrt(column_sums) + 1e-08)
    return (momentum_next, left_factor, right_factor)


def solution(mesh):
    wide = mesh.shape["col"] * mesh.shape["rep"]
    tall = mesh.shape["row"]
    placed = (P("row", WIDE), P("row", WIDE), P(WIDE, None))

    def run(momentum, gradient, right_prev):
        return local(wide, tall, momentum, gradient, right_prev)

    return jax.shard_map(
        run,
        mesh=mesh,
        in_specs=placed,
        out_specs=(P("row", WIDE), P("row", None), P(WIDE, None)),
        check_vma=False,
    )
```

```python
import jax
import jax.numpy as jnp
from jax import lax
from jax.experimental import pallas as pl
from jax.experimental.pallas import tpu as pltpu
from jax.sharding import PartitionSpec as P

RANK = 256
BLOCK = 64
SPAN = 64
WIDE = ("col", "rep")


def dot32(a, b, a_dim, b_dim):
    return lax.dot_general(
        a,
        b,
        (((a_dim,), (b_dim,)), ((), ())),
        precision=lax.Precision.HIGHEST,
        preferred_element_type=jnp.float32,
    )


def eliminate(rows, offset, sub):
    count = len(rows)
    done = []
    for group in range(count):
        first = offset + 8 * group
        cols = [
            [
                jnp.broadcast_to(rows[r][:, first + k : first + k + 1], (8, 128))
                for k in range(8)
            ]
            for r in range(group, count)
        ]
        scale = jnp.zeros((8, 128), jnp.float32)
        for k in range(8):
            pivot = jnp.broadcast_to(cols[0][k][k : k + 1, :], (8, 128))
            inverse = 1.0 / pivot
            scale = jnp.where(sub == k, lax.rsqrt(pivot), scale)
            pivot_row = jnp.broadcast_to(rows[group][k : k + 1, :], (8, 128)) * inverse
            pivot_cols = [
                jnp.broadcast_to(cols[0][j][k : k + 1, :], (8, 128)) * inverse
                for j in range(k + 1, 8)
            ]
            for r in range(group, count):
                factor = cols[r - group][k]
                if r == group:
                    if k == 7:
                        continue
                    factor = jnp.where(sub > k, factor, 0.0)
                rows[r] = rows[r] - factor * pivot_row
                for j in range(k + 1, 8):
                    cols[r - group][j] = cols[r - group][j] - factor * pivot_cols[j - k - 1]
        done.append(rows[group] * scale)
    return done


def inverse_factor_kernel(gram_ref, out_ref, rest_ref):
    sub = lax.broadcasted_iota(jnp.int32, (8, 128), 0)
    lane = lax.broadcasted_iota(jnp.int32, (8, 128), 1)
    rest_ref[...] = gram_ref[...]
    out_ref[...] = jnp.zeros((RANK, RANK), jnp.float32)
    for low in range(0, RANK, BLOCK):
        high = low + BLOCK
        base = low // 128 * 128
        offset = low - base
        other = BLOCK - offset
        rows = []
        for r in range(BLOCK // 8):
            held = rest_ref[low + 8 * r : low + 8 * r + 8, base : base + 128]
            unit = jnp.where(lane == other + 8 * r + sub, 1.0, 0.0)
            rows.append(jnp.where((lane >= offset) & (lane < offset + BLOCK), held, unit))
        block = jnp.concatenate(eliminate(rows, offset, sub), axis=0)
        inverse = block[:, other : other + BLOCK]
        if low:
            out_ref[low:high, 0:low] = dot32(inverse, out_ref[low:high, 0:low], 1, 0)
        out_ref[low:high, low:high] = inverse
        if high < RANK:
            upper = dot32(inverse, rest_ref[low:high, high:RANK], 1, 0)
            solved = out_ref[low:high, 0:high]
            rest_ref[high:RANK, high:RANK] = rest_ref[high:RANK, high:RANK] - dot32(
                upper, upper, 0, 0
            )
            out_ref[high:RANK, 0:high] = out_ref[high:RANK, 0:high] - dot32(upper, solved, 0, 0)


def inverse_factor(gram_matrix):
    return pl.pallas_call(
        inverse_factor_kernel,
        out_shape=jax.ShapeDtypeStruct((RANK, RANK), jnp.float32),
        in_specs=[pl.BlockSpec(memory_space=pltpu.VMEM)],
        out_specs=pl.BlockSpec(memory_space=pltpu.VMEM),
        scratch_shapes=[pltpu.VMEM((RANK, RANK), jnp.float32)],
        cost_estimate=pl.CostEstimate(flops=400_000_000, bytes_accessed=524288, transcendentals=0),
        name="inverse_factor",
    )(gram_matrix)


def scatter_sum(x, axes, count):
    parts = x.reshape(count, x.shape[0] // count, x.shape[1])
    return jnp.sum(lax.all_to_all(parts, axes, 0, 0, tiled=True), axis=0)


def gather(x, axes, count):
    return lax.all_to_all(
        jnp.broadcast_to(x[None], (count,) + x.shape), axes, 0, 0, tiled=True
    )


def project_kernel(buffer_ref, left_ref, gram_ref, out_ref):
    left = left_ref[...]
    high = left.astype(jnp.bfloat16)
    rest = left - high.astype(jnp.float32)
    middle = rest.astype(jnp.bfloat16)
    low = (rest - middle.astype(jnp.float32)).astype(jnp.bfloat16)
    far, near = buffer_ref.shape[1] // SPAN // out_ref.shape[0], out_ref.shape[0]
    for i in range(far):
        block = buffer_ref[:, i * near * SPAN : (i + 1) * near * SPAN]
        part = sum(
            lax.dot_general(
                block, piece, (((0,), (0,)), ((), ())), preferred_element_type=jnp.float32
            )
            for piece in (low, middle, high)
        )
        for j in range(near):
            out_ref[j, i * SPAN : (i + 1) * SPAN, :] = part[j * SPAN : (j + 1) * SPAN, :]
    for j in range(near):
        out_ref[j, far * SPAN :, :] = gram_ref[...]


def project(buffer, left_raw, gram_rows, near):
    columns = buffer.shape[1]
    share = gram_rows.shape[0]
    return pl.pallas_call(
        project_kernel,
        out_shape=jax.ShapeDtypeStruct((near, columns // near + share, RANK), jnp.float32),
        in_specs=[pl.BlockSpec(memory_space=pltpu.VMEM)] * 3,
        out_specs=pl.BlockSpec(memory_space=pltpu.VMEM),
        compiler_params=pltpu.CompilerParams(vmem_limit_bytes=32 * 1024 * 1024),
        cost_estimate=pl.CostEstimate(
            flops=6 * buffer.size * RANK, bytes_accessed=3_000_000, transcendentals=0
        ),
        name="project",
    )(buffer, left_raw, gram_rows)


def local(wide, tall, momentum, gradient, right_prev):
    place = lax.axis_index(WIDE)
    near = 4
    far = tall // near
    adjacent = [[i * near + j for j in range(near)] for i in range(far)]
    strided = [[i * near + j for i in range(far)] for j in range(near)]
    buffer = (momentum.astype(jnp.float32) + gradient.astype(jnp.float32)).astype(jnp.bfloat16)
    left_partial = jnp.dot(buffer, right_prev, preferred_element_type=jnp.float32)
    rows = left_partial.shape[0]
    left_rows = scatter_sum(left_partial, WIDE, wide)
    left_raw = gather(left_rows, WIDE, wide).reshape(rows, RANK)

    share = RANK // wide
    own = lax.dynamic_slice(left_raw, (0, place * share), (rows, share))
    blocks = project(buffer, left_raw, dot32(own, left_raw, 0, 0), near)
    blocks = lax.all_to_all(blocks, "row", 0, 0, axis_index_groups=adjacent, tiled=True)
    summed = jnp.sum(blocks, axis=0)
    blocks = jnp.concatenate(
        [
            summed[: far * SPAN].reshape(far, SPAN, RANK),
            jnp.broadcast_to(summed[None, far * SPAN :], (far, share, RANK)),
        ],
        axis=1,
    )
    blocks = lax.all_to_all(blocks, "row", 0, 0, axis_index_groups=strided, tiled=True)
    right_raw = jnp.sum(blocks[:, :SPAN], axis=0)
    gram_rows = jnp.sum(blocks[:, SPAN:], axis=0)
    gram_matrix = gather(gram_rows, WIDE, wide).reshape(RANK, RANK)
    inverse = inverse_factor(gram_matrix)

    left_factor = dot32(left_raw, inverse, 1, 1)
    left_low = left_factor.astype(jnp.bfloat16)
    right_rows = dot32(right_raw, inverse, 1, 1).astype(jnp.bfloat16)
    right_low = lax.all_gather(right_rows, "row", axis=0, tiled=True)
    right_wide = right_low.astype(jnp.float32)
    own_sums = jnp.sum(right_wide * right_wide, axis=0, keepdims=True)
    column_sums = jnp.sum(gather(own_sums, WIDE, wide), axis=0)
    outer = lax.dot_general(
        left_low, right_low, (((1,), (1,)), ((), ())), preferred_element_type=jnp.float32
    )
    momentum_next = (buffer.astype(jnp.float32) - 0.1 * outer).astype(jnp.bfloat16)
    right_factor = right_wide / (jnp.sqrt(column_sums) + 1e-08)
    return (momentum_next, left_factor, right_factor)


def solution(mesh):
    wide = mesh.shape["col"] * mesh.shape["rep"]
    tall = mesh.shape["row"]
    placed = (P("row", WIDE), P("row", WIDE), P(WIDE, None))

    def run(momentum, gradient, right_prev):
        return local(wide, tall, momentum, gradient, right_prev)

    return jax.shard_map(
        run,
        mesh=mesh,
        in_specs=placed,
        out_specs=(P("row", WIDE), P("row", None), P(WIDE, None)),
        check_vma=False,
    )
```

```python
import jax
import jax.numpy as jnp
from jax import lax
from jax.experimental import pallas as pl
from jax.experimental.pallas import tpu as pltpu
from jax.sharding import PartitionSpec as P

RANK = 256
BLOCK = 64
SPAN = 64
WIDE = ("col", "rep")


def dot32(a, b, a_dim, b_dim):
    return lax.dot_general(
        a,
        b,
        (((a_dim,), (b_dim,)), ((), ())),
        precision=lax.Precision.HIGHEST,
        preferred_element_type=jnp.float32,
    )


def eliminate(rows, offset, sub):
    count = len(rows)
    done = []
    for group in range(count):
        first = offset + 8 * group
        cols = [
            [
                jnp.broadcast_to(rows[r][:, first + k : first + k + 1], (8, 128))
                for k in range(8)
            ]
            for r in range(group, count)
        ]
        scale = jnp.zeros((8, 128), jnp.float32)
        for k in range(8):
            pivot = jnp.broadcast_to(cols[0][k][k : k + 1, :], (8, 128))
            inverse = 1.0 / pivot
            scale = jnp.where(sub == k, lax.rsqrt(pivot), scale)
            pivot_row = jnp.broadcast_to(rows[group][k : k + 1, :], (8, 128)) * inverse
            pivot_cols = [
                jnp.broadcast_to(cols[0][j][k : k + 1, :], (8, 128)) * inverse
                for j in range(k + 1, 8)
            ]
            for r in range(group, count):
                factor = cols[r - group][k]
                if r == group:
                    if k == 7:
                        continue
                    factor = jnp.where(sub > k, factor, 0.0)
                rows[r] = rows[r] - factor * pivot_row
                for j in range(k + 1, 8):
                    cols[r - group][j] = cols[r - group][j] - factor * pivot_cols[j - k - 1]
        done.append(rows[group] * scale)
    return done


def inverse_factor_kernel(gram_ref, out_ref, rest_ref):
    sub = lax.broadcasted_iota(jnp.int32, (8, 128), 0)
    lane = lax.broadcasted_iota(jnp.int32, (8, 128), 1)
    rest_ref[...] = gram_ref[...]
    out_ref[...] = jnp.zeros((RANK, RANK), jnp.float32)
    for low in range(0, RANK, BLOCK):
        high = low + BLOCK
        base = low // 128 * 128
        offset = low - base
        other = BLOCK - offset
        rows = []
        for r in range(BLOCK // 8):
            held = rest_ref[low + 8 * r : low + 8 * r + 8, base : base + 128]
            unit = jnp.where(lane == other + 8 * r + sub, 1.0, 0.0)
            rows.append(jnp.where((lane >= offset) & (lane < offset + BLOCK), held, unit))
        block = jnp.concatenate(eliminate(rows, offset, sub), axis=0)
        inverse = block[:, other : other + BLOCK]
        if low:
            out_ref[low:high, 0:low] = dot32(inverse, out_ref[low:high, 0:low], 1, 0)
        out_ref[low:high, low:high] = inverse
        if high < RANK:
            upper = dot32(inverse, rest_ref[low:high, high:RANK], 1, 0)
            solved = out_ref[low:high, 0:high]
            rest_ref[high:RANK, high:RANK] = rest_ref[high:RANK, high:RANK] - dot32(
                upper, upper, 0, 0
            )
            out_ref[high:RANK, 0:high] = out_ref[high:RANK, 0:high] - dot32(upper, solved, 0, 0)


def inverse_factor(gram_matrix):
    return pl.pallas_call(
        inverse_factor_kernel,
        out_shape=jax.ShapeDtypeStruct((RANK, RANK), jnp.float32),
        in_specs=[pl.BlockSpec(memory_space=pltpu.VMEM)],
        out_specs=pl.BlockSpec(memory_space=pltpu.VMEM),
        scratch_shapes=[pltpu.VMEM((RANK, RANK), jnp.float32)],
        cost_estimate=pl.CostEstimate(flops=400_000_000, bytes_accessed=524288, transcendentals=0),
        name="inverse_factor",
    )(gram_matrix)


def scatter_sum(x, axes, count):
    parts = x.reshape(count, x.shape[0] // count, x.shape[1])
    return jnp.sum(lax.all_to_all(parts, axes, 0, 0, tiled=True), axis=0)


def gather(x, axes, count):
    return lax.all_to_all(
        jnp.broadcast_to(x[None], (count,) + x.shape), axes, 0, 0, tiled=True
    )


def project_kernel(buffer_ref, left_ref, out_ref):
    left = left_ref[...]
    high = left.astype(jnp.bfloat16)
    rest = left - high.astype(jnp.float32)
    middle = rest.astype(jnp.bfloat16)
    low = (rest - middle.astype(jnp.float32)).astype(jnp.bfloat16)
    far, near = buffer_ref.shape[1] // SPAN // out_ref.shape[0], out_ref.shape[0]
    for i in range(far):
        block = buffer_ref[:, i * near * SPAN : (i + 1) * near * SPAN]
        part = sum(
            lax.dot_general(
                block, piece, (((0,), (0,)), ((), ())), preferred_element_type=jnp.float32
            )
            for piece in (low, middle, high)
        )
        for j in range(near):
            out_ref[j, i * SPAN : (i + 1) * SPAN, :] = part[j * SPAN : (j + 1) * SPAN, :]


def project(buffer, left_raw, near):
    columns = buffer.shape[1]
    return pl.pallas_call(
        project_kernel,
        out_shape=jax.ShapeDtypeStruct((near, columns // near, RANK), jnp.float32),
        in_specs=[pl.BlockSpec(memory_space=pltpu.VMEM)] * 2,
        out_specs=pl.BlockSpec(memory_space=pltpu.VMEM),
        compiler_params=pltpu.CompilerParams(vmem_limit_bytes=32 * 1024 * 1024),
        cost_estimate=pl.CostEstimate(
            flops=6 * buffer.size * RANK, bytes_accessed=3_000_000, transcendentals=0
        ),
        name="project",
    )(buffer, left_raw)


def local(wide, tall, momentum, gradient, right_prev):
    place = lax.axis_index(WIDE)
    near = 4
    far = tall // near
    adjacent = [[i * near + j for j in range(near)] for i in range(far)]
    strided = [[i * near + j for i in range(far)] for j in range(near)]
    buffer = (momentum.astype(jnp.float32) + gradient.astype(jnp.float32)).astype(jnp.bfloat16)
    left_partial = jnp.dot(buffer, right_prev, preferred_element_type=jnp.float32)
    rows = left_partial.shape[0]
    left_rows = scatter_sum(left_partial, WIDE, wide)
    left_raw = gather(left_rows, WIDE, wide).reshape(rows, RANK)

    share = RANK // wide
    own = lax.dynamic_slice(left_raw, (0, place * share), (rows, share))
    gram_rows = jnp.sum(gather(dot32(own, left_raw, 0, 0), "row", tall), axis=0)
    blocks = project(buffer, left_raw, near)

    gram_rows, blocks = lax.optimization_barrier((gram_rows, blocks))
    blocks = lax.all_to_all(blocks, "row", 0, 0, axis_index_groups=adjacent, tiled=True)
    gram_matrix = lax.all_gather(gram_rows, "rep", axis=0, tiled=True)
    gram_matrix = lax.all_gather(
        gram_matrix, "col", axis=0, axis_index_groups=[[0, 1], [2, 3], [4, 5], [6, 7]], tiled=True
    )
    gram_matrix = lax.all_gather(
        gram_matrix, "col", axis=0, axis_index_groups=[[0, 2, 4, 6], [1, 3, 5, 7]], tiled=True
    )
    blocks = jnp.sum(blocks, axis=0).reshape(far, SPAN, RANK)

    gram_matrix, blocks = lax.optimization_barrier((gram_matrix, blocks))
    blocks = lax.all_to_all(blocks, "row", 0, 0, axis_index_groups=strided, tiled=True)
    inverse = inverse_factor(gram_matrix)
    right_raw = jnp.sum(blocks, axis=0)

    left_factor = dot32(left_raw, inverse, 1, 1)
    left_low = left_factor.astype(jnp.bfloat16)
    right_rows = dot32(right_raw, inverse, 1, 1).astype(jnp.bfloat16)
    right_low = lax.all_gather(right_rows, "row", axis=0, tiled=True)
    right_wide = right_low.astype(jnp.float32)
    own_sums = jnp.sum(right_wide * right_wide, axis=0, keepdims=True)
    column_sums = jnp.sum(gather(own_sums, WIDE, wide), axis=0)
    outer = lax.dot_general(
        left_low, right_low, (((1,), (1,)), ((), ())), preferred_element_type=jnp.float32
    )
    momentum_next = (buffer.astype(jnp.float32) - 0.1 * outer).astype(jnp.bfloat16)
    right_factor = right_wide / (jnp.sqrt(column_sums) + 1e-08)
    return (momentum_next, left_factor, right_factor)


def solution(mesh):
    wide = mesh.shape["col"] * mesh.shape["rep"]
    tall = mesh.shape["row"]
    placed = (P("row", WIDE), P("row", WIDE), P(WIDE, None))

    def run(momentum, gradient, right_prev):
        return local(wide, tall, momentum, gradient, right_prev)

    return jax.shard_map(
        run,
        mesh=mesh,
        in_specs=placed,
        out_specs=(P("row", WIDE), P("row", None), P(WIDE, None)),
        check_vma=False,
    )
```

```python
import jax
import jax.numpy as jnp
from jax import lax
from jax.experimental import pallas as pl
from jax.experimental.pallas import tpu as pltpu
from jax.sharding import PartitionSpec as P

RANK = 256
BLOCK = 64
SPAN = 64
NEAR = 4
WIDE = ("col", "rep")


def dot32(a, b, a_dim, b_dim):
    return lax.dot_general(
        a,
        b,
        (((a_dim,), (b_dim,)), ((), ())),
        precision=lax.Precision.HIGHEST,
        preferred_element_type=jnp.float32,
    )


def eliminate(rows, offset, sub):
    count = len(rows)
    done = []
    for group in range(count):
        first = offset + 8 * group
        cols = [
            [
                jnp.broadcast_to(rows[r][:, first + k : first + k + 1], (8, 128))
                for k in range(8)
            ]
            for r in range(group, count)
        ]
        scale = jnp.zeros((8, 128), jnp.float32)
        for k in range(8):
            pivot = jnp.broadcast_to(cols[0][k][k : k + 1, :], (8, 128))
            inverse = 1.0 / pivot
            scale = jnp.where(sub == k, lax.rsqrt(pivot), scale)
            pivot_row = jnp.broadcast_to(rows[group][k : k + 1, :], (8, 128)) * inverse
            pivot_cols = [
                jnp.broadcast_to(cols[0][j][k : k + 1, :], (8, 128)) * inverse
                for j in range(k + 1, 8)
            ]
            for r in range(group, count):
                factor = cols[r - group][k]
                if r == group:
                    if k == 7:
                        continue
                    factor = jnp.where(sub > k, factor, 0.0)
                rows[r] = rows[r] - factor * pivot_row
                for j in range(k + 1, 8):
                    cols[r - group][j] = cols[r - group][j] - factor * pivot_cols[j - k - 1]
        done.append(rows[group] * scale)
    return done


def inverse_factor_kernel(gram_ref, out_ref, rest_ref):
    sub = lax.broadcasted_iota(jnp.int32, (8, 128), 0)
    lane = lax.broadcasted_iota(jnp.int32, (8, 128), 1)
    rest_ref[...] = gram_ref[...]
    out_ref[...] = jnp.zeros((RANK, RANK), jnp.float32)
    for low in range(0, RANK, BLOCK):
        high = low + BLOCK
        base = low // 128 * 128
        offset = low - base
        other = BLOCK - offset
        rows = []
        for r in range(BLOCK // 8):
            held = rest_ref[low + 8 * r : low + 8 * r + 8, base : base + 128]
            unit = jnp.where(lane == other + 8 * r + sub, 1.0, 0.0)
            rows.append(jnp.where((lane >= offset) & (lane < offset + BLOCK), held, unit))
        block = jnp.concatenate(eliminate(rows, offset, sub), axis=0)
        inverse = block[:, other : other + BLOCK]
        if low:
            out_ref[low:high, 0:low] = dot32(inverse, out_ref[low:high, 0:low], 1, 0)
        out_ref[low:high, low:high] = inverse
        if high < RANK:
            upper = dot32(inverse, rest_ref[low:high, high:RANK], 1, 0)
            solved = out_ref[low:high, 0:high]
            rest_ref[high:RANK, high:RANK] = rest_ref[high:RANK, high:RANK] - dot32(
                upper, upper, 0, 0
            )
            out_ref[high:RANK, 0:high] = out_ref[high:RANK, 0:high] - dot32(upper, solved, 0, 0)


def inverse_factor(gram_matrix):
    return pl.pallas_call(
        inverse_factor_kernel,
        out_shape=jax.ShapeDtypeStruct((RANK, RANK), jnp.float32),
        in_specs=[pl.BlockSpec(memory_space=pltpu.VMEM)],
        out_specs=pl.BlockSpec(memory_space=pltpu.VMEM),
        scratch_shapes=[pltpu.VMEM((RANK, RANK), jnp.float32)],
        cost_estimate=pl.CostEstimate(flops=400_000_000, bytes_accessed=524288, transcendentals=0),
        name="inverse_factor",
    )(gram_matrix)


def scatter_sum(x, axes, count):
    parts = x.reshape(count, x.shape[0] // count, x.shape[1])
    return jnp.sum(lax.all_to_all(parts, axes, 0, 0, tiled=True), axis=0)


def gather(x, axes, count):
    return lax.all_to_all(
        jnp.broadcast_to(x[None], (count,) + x.shape), axes, 0, 0, tiled=True
    )


def project_kernel(near_ref, buffer_ref, left_ref, *refs):
    out_refs, part_ref = refs[:-1], refs[-1]
    left = left_ref[...]
    high = left.astype(jnp.bfloat16)
    rest = left - high.astype(jnp.float32)
    middle = rest.astype(jnp.bfloat16)
    low = (rest - middle.astype(jnp.float32)).astype(jnp.bfloat16)
    own = near_ref[0]
    for i in range(buffer_ref.shape[1] // RANK):
        block = buffer_ref[:, i * RANK : (i + 1) * RANK]
        part_ref[i] = sum(
            lax.dot_general(
                block, piece, (((0,), (0,)), ((), ())), preferred_element_type=jnp.float32
            )
            for piece in (low, middle, high)
        )
        for shift in range(NEAR):
            start = pl.multiple_of(lax.rem(own + shift, NEAR) * SPAN, SPAN)
            out_refs[shift][i * SPAN : (i + 1) * SPAN, :] = part_ref[i, pl.ds(start, SPAN), :]


def project(buffer, left_raw, own):
    columns = buffer.shape[1]
    return pl.pallas_call(
        project_kernel,
        out_shape=[jax.ShapeDtypeStruct((columns // NEAR, RANK), jnp.float32)] * NEAR,
        in_specs=[pl.BlockSpec(memory_space=pltpu.SMEM)]
        + [pl.BlockSpec(memory_space=pltpu.VMEM)] * 2,
        out_specs=[pl.BlockSpec(memory_space=pltpu.VMEM)] * NEAR,
        scratch_shapes=[pltpu.VMEM((columns // RANK, RANK, RANK), jnp.float32)],
        compiler_params=pltpu.CompilerParams(vmem_limit_bytes=32 * 1024 * 1024),
        cost_estimate=pl.CostEstimate(
            flops=6 * buffer.size * RANK, bytes_accessed=3_000_000, transcendentals=0
        ),
        name="project",
    )(own.reshape(1), buffer, left_raw)


def local(wide, tall, momentum, gradient, right_prev):
    place = lax.axis_index(WIDE)
    far = tall // NEAR
    strided = [[i * NEAR + j for i in range(far)] for j in range(NEAR)]
    buffer = (momentum.astype(jnp.float32) + gradient.astype(jnp.float32)).astype(jnp.bfloat16)
    left_partial = jnp.dot(buffer, right_prev, preferred_element_type=jnp.float32)
    rows = left_partial.shape[0]
    left_rows = scatter_sum(left_partial, WIDE, wide)
    left_raw = gather(left_rows, WIDE, wide).reshape(rows, RANK)

    share = RANK // wide
    own = lax.dynamic_slice(left_raw, (0, place * share), (rows, share))
    gram_rows = jnp.sum(gather(dot32(own, left_raw, 0, 0), "row", tall), axis=0)
    blocks = project(buffer, left_raw, lax.rem(lax.axis_index("row"), NEAR))

    gram_rows, *blocks = lax.optimization_barrier((gram_rows, *blocks))
    for shift in range(1, NEAR):
        ring = [(i, i // NEAR * NEAR + (i + shift) % NEAR) for i in range(tall)]
        blocks[shift] = lax.ppermute(blocks[shift], "row", ring)
    gram_matrix = gather(gram_rows, WIDE, wide).reshape(RANK, RANK)
    blocks = sum(blocks).reshape(far, SPAN, RANK)

    gram_matrix, blocks = lax.optimization_barrier((gram_matrix, blocks))
    blocks = lax.all_to_all(blocks, "row", 0, 0, axis_index_groups=strided, tiled=True)
    inverse = inverse_factor(gram_matrix)
    right_raw = jnp.sum(blocks, axis=0)

    left_factor = dot32(left_raw, inverse, 1, 1)
    left_low = left_factor.astype(jnp.bfloat16)
    right_rows = dot32(right_raw, inverse, 1, 1).astype(jnp.bfloat16)
    right_low = lax.all_gather(right_rows, "row", axis=0, tiled=True)
    right_wide = right_low.astype(jnp.float32)
    own_sums = jnp.sum(right_wide * right_wide, axis=0, keepdims=True)
    column_sums = jnp.sum(gather(own_sums, WIDE, wide), axis=0)
    outer = lax.dot_general(
        left_low, right_low, (((1,), (1,)), ((), ())), preferred_element_type=jnp.float32
    )
    momentum_next = (buffer.astype(jnp.float32) - 0.1 * outer).astype(jnp.bfloat16)
    right_factor = right_wide / (jnp.sqrt(column_sums) + 1e-08)
    return (momentum_next, left_factor, right_factor)


def solution(mesh):
    wide = mesh.shape["col"] * mesh.shape["rep"]
    tall = mesh.shape["row"]
    placed = (P("row", WIDE), P("row", WIDE), P(WIDE, None))

    def run(momentum, gradient, right_prev):
        return local(wide, tall, momentum, gradient, right_prev)

    return jax.shard_map(
        run,
        mesh=mesh,
        in_specs=placed,
        out_specs=(P("row", WIDE), P("row", None), P(WIDE, None)),
        check_vma=False,
    )
```

```python
import jax
import jax.numpy as jnp
from jax import lax
from jax.experimental import pallas as pl
from jax.experimental.pallas import tpu as pltpu
from jax.sharding import PartitionSpec as P

RANK = 256
BLOCK = 64
NEAR = 4
WIDE = ("col", "rep")


def dot32(a, b, a_dim, b_dim):
    return lax.dot_general(
        a,
        b,
        (((a_dim,), (b_dim,)), ((), ())),
        precision=lax.Precision.HIGHEST,
        preferred_element_type=jnp.float32,
    )


def eliminate(rows, offset, sub):
    count = len(rows)
    done = []
    for group in range(count):
        first = offset + 8 * group
        cols = [
            [
                jnp.broadcast_to(rows[r][:, first + k : first + k + 1], (8, 128))
                for k in range(8)
            ]
            for r in range(group, count)
        ]
        scale = jnp.zeros((8, 128), jnp.float32)
        for k in range(8):
            pivot = jnp.broadcast_to(cols[0][k][k : k + 1, :], (8, 128))
            inverse = 1.0 / pivot
            scale = jnp.where(sub == k, lax.rsqrt(pivot), scale)
            pivot_row = jnp.broadcast_to(rows[group][k : k + 1, :], (8, 128)) * inverse
            pivot_cols = [
                jnp.broadcast_to(cols[0][j][k : k + 1, :], (8, 128)) * inverse
                for j in range(k + 1, 8)
            ]
            for r in range(group, count):
                factor = cols[r - group][k]
                if r == group:
                    if k == 7:
                        continue
                    factor = jnp.where(sub > k, factor, 0.0)
                rows[r] = rows[r] - factor * pivot_row
                for j in range(k + 1, 8):
                    cols[r - group][j] = cols[r - group][j] - factor * pivot_cols[j - k - 1]
        done.append(rows[group] * scale)
    return done


def inverse_factor_kernel(gram_ref, out_ref, rest_ref):
    sub = lax.broadcasted_iota(jnp.int32, (8, 128), 0)
    lane = lax.broadcasted_iota(jnp.int32, (8, 128), 1)
    rest_ref[...] = gram_ref[...]
    out_ref[...] = jnp.zeros((RANK, RANK), jnp.float32)
    for low in range(0, RANK, BLOCK):
        high = low + BLOCK
        base = low // 128 * 128
        offset = low - base
        other = BLOCK - offset
        rows = []
        for r in range(BLOCK // 8):
            held = rest_ref[low + 8 * r : low + 8 * r + 8, base : base + 128]
            unit = jnp.where(lane == other + 8 * r + sub, 1.0, 0.0)
            rows.append(jnp.where((lane >= offset) & (lane < offset + BLOCK), held, unit))
        block = jnp.concatenate(eliminate(rows, offset, sub), axis=0)
        inverse = block[:, other : other + BLOCK]
        if low:
            out_ref[low:high, 0:low] = dot32(inverse, out_ref[low:high, 0:low], 1, 0)
        out_ref[low:high, low:high] = inverse
        if high < RANK:
            upper = dot32(inverse, rest_ref[low:high, high:RANK], 1, 0)
            solved = out_ref[low:high, 0:high]
            rest_ref[high:RANK, high:RANK] = rest_ref[high:RANK, high:RANK] - dot32(
                upper, upper, 0, 0
            )
            out_ref[high:RANK, 0:high] = out_ref[high:RANK, 0:high] - dot32(upper, solved, 0, 0)


def inverse_factor(gram_matrix):
    return pl.pallas_call(
        inverse_factor_kernel,
        out_shape=jax.ShapeDtypeStruct((RANK, RANK), jnp.float32),
        in_specs=[pl.BlockSpec(memory_space=pltpu.VMEM)],
        out_specs=pl.BlockSpec(memory_space=pltpu.VMEM),
        scratch_shapes=[pltpu.VMEM((RANK, RANK), jnp.float32)],
        cost_estimate=pl.CostEstimate(flops=400_000_000, bytes_accessed=524288, transcendentals=0),
        name="inverse_factor",
    )(gram_matrix)


def scatter_sum(x, axes, count):
    parts = x.reshape(count, x.shape[0] // count, x.shape[1])
    return jnp.sum(lax.all_to_all(parts, axes, 0, 0, tiled=True), axis=0)


def gather(x, axes, count):
    return lax.all_to_all(
        jnp.broadcast_to(x[None], (count,) + x.shape), axes, 0, 0, tiled=True
    )


def project_kernel(near_ref, buffer_ref, left_ref, *out_refs):
    left = left_ref[...]
    high = left.astype(jnp.bfloat16)
    rest = left - high.astype(jnp.float32)
    middle = rest.astype(jnp.bfloat16)
    low = (rest - middle.astype(jnp.float32)).astype(jnp.bfloat16)
    count = len(out_refs)
    span = buffer_ref.shape[1] // count
    for shift in range(count):
        start = pl.multiple_of(lax.rem(near_ref[0] + shift, count) * span, span)
        block = buffer_ref[:, pl.ds(start, span)]
        out_refs[shift][...] = sum(
            lax.dot_general(
                block, piece, (((0,), (0,)), ((), ())), preferred_element_type=jnp.float32
            )
            for piece in (low, middle, high)
        )


def project(buffer, left_raw, own):
    columns = buffer.shape[1]
    return pl.pallas_call(
        project_kernel,
        out_shape=[jax.ShapeDtypeStruct((columns // NEAR, RANK), jnp.float32)] * NEAR,
        in_specs=[pl.BlockSpec(memory_space=pltpu.SMEM)]
        + [pl.BlockSpec(memory_space=pltpu.VMEM)] * 2,
        out_specs=[pl.BlockSpec(memory_space=pltpu.VMEM)] * NEAR,
        compiler_params=pltpu.CompilerParams(vmem_limit_bytes=32 * 1024 * 1024),
        cost_estimate=pl.CostEstimate(
            flops=6 * buffer.size * RANK, bytes_accessed=3_000_000, transcendentals=0
        ),
        name="project",
    )(own.reshape(1), buffer, left_raw)


def local(wide, tall, momentum, gradient, right_prev):
    place = lax.axis_index(WIDE)
    far = tall // NEAR
    adjacent = [[i * NEAR + j for j in range(NEAR)] for i in range(far)]
    strided = [[i * NEAR + j for i in range(far)] for j in range(NEAR)]
    buffer = (momentum.astype(jnp.float32) + gradient.astype(jnp.float32)).astype(jnp.bfloat16)
    left_partial = jnp.dot(buffer, right_prev, preferred_element_type=jnp.float32)
    rows = left_partial.shape[0]
    left_rows = scatter_sum(left_partial, WIDE, wide)
    left_raw = gather(left_rows, WIDE, wide).reshape(rows, RANK)

    share = RANK // wide
    own = lax.dynamic_slice(left_raw, (0, place * share), (rows, share))
    gram_rows = jnp.sum(gather(dot32(own, left_raw, 0, 0), "row", tall), axis=0)
    blocks = project(buffer, left_raw, lax.rem(lax.axis_index("row"), NEAR))

    gram_rows, *blocks = lax.optimization_barrier((gram_rows, *blocks))
    gram_matrix = gather(gram_rows, WIDE, wide).reshape(RANK, RANK)
    for shift in range(1, NEAR):
        ring = [(i, i // NEAR * NEAR + (i + shift) % NEAR) for i in range(tall)]
        blocks[shift] = lax.ppermute(blocks[shift], "row", ring)
    inverse = inverse_factor(gram_matrix)

    left_factor = dot32(left_raw, inverse, 1, 1)
    left_low = left_factor.astype(jnp.bfloat16)
    part = dot32(sum(blocks), inverse, 1, 1).astype(jnp.bfloat16)
    parts = lax.all_to_all(
        jnp.broadcast_to(part[None], (far,) + part.shape),
        "row",
        0,
        0,
        axis_index_groups=strided,
        tiled=True,
    )
    right_rows = jnp.sum(parts.astype(jnp.float32), axis=0).astype(jnp.bfloat16)
    right_low = lax.all_gather(
        right_rows, "row", axis=0, axis_index_groups=adjacent, tiled=True
    )
    right_wide = right_low.astype(jnp.float32)
    own_sums = jnp.sum(right_wide * right_wide, axis=0, keepdims=True)
    column_sums = jnp.sum(gather(own_sums, WIDE, wide), axis=0)
    outer = lax.dot_general(
        left_low, right_low, (((1,), (1,)), ((), ())), preferred_element_type=jnp.float32
    )
    momentum_next = (buffer.astype(jnp.float32) - 0.1 * outer).astype(jnp.bfloat16)
    right_factor = right_wide / (jnp.sqrt(column_sums) + 1e-08)
    return (momentum_next, left_factor, right_factor)


def solution(mesh):
    wide = mesh.shape["col"] * mesh.shape["rep"]
    tall = mesh.shape["row"]
    placed = (P("row", WIDE), P("row", WIDE), P(WIDE, None))

    def run(momentum, gradient, right_prev):
        return local(wide, tall, momentum, gradient, right_prev)

    return jax.shard_map(
        run,
        mesh=mesh,
        in_specs=placed,
        out_specs=(P("row", WIDE), P("row", None), P(WIDE, None)),
        check_vma=False,
    )
```

```python
import jax
import jax.numpy as jnp
from jax import lax
from jax.experimental import pallas as pl
from jax.experimental.pallas import tpu as pltpu
from jax.sharding import PartitionSpec as P

RANK = 256
BLOCK = 64
SPAN = 64
NEAR = 4
WIDE = ("col", "rep")


def dot32(a, b, a_dim, b_dim):
    return lax.dot_general(
        a,
        b,
        (((a_dim,), (b_dim,)), ((), ())),
        precision=lax.Precision.HIGHEST,
        preferred_element_type=jnp.float32,
    )


def eliminate(rows, offset, sub):
    count = len(rows)
    done = []
    for group in range(count):
        first = offset + 8 * group
        cols = [
            [
                jnp.broadcast_to(rows[r][:, first + k : first + k + 1], (8, 128))
                for k in range(8)
            ]
            for r in range(group, count)
        ]
        scale = jnp.zeros((8, 128), jnp.float32)
        for k in range(8):
            pivot = jnp.broadcast_to(cols[0][k][k : k + 1, :], (8, 128))
            inverse = 1.0 / pivot
            scale = jnp.where(sub == k, lax.rsqrt(pivot), scale)
            pivot_row = jnp.broadcast_to(rows[group][k : k + 1, :], (8, 128)) * inverse
            pivot_cols = [
                jnp.broadcast_to(cols[0][j][k : k + 1, :], (8, 128)) * inverse
                for j in range(k + 1, 8)
            ]
            for r in range(group, count):
                factor = cols[r - group][k]
                if r == group:
                    if k == 7:
                        continue
                    factor = jnp.where(sub > k, factor, 0.0)
                rows[r] = rows[r] - factor * pivot_row
                for j in range(k + 1, 8):
                    cols[r - group][j] = cols[r - group][j] - factor * pivot_cols[j - k - 1]
        done.append(rows[group] * scale)
    return done


def inverse_factor_kernel(gram_ref, out_ref, rest_ref):
    sub = lax.broadcasted_iota(jnp.int32, (8, 128), 0)
    lane = lax.broadcasted_iota(jnp.int32, (8, 128), 1)
    rest_ref[...] = gram_ref[...]
    out_ref[...] = jnp.zeros((RANK, RANK), jnp.float32)
    for low in range(0, RANK, BLOCK):
        high = low + BLOCK
        base = low // 128 * 128
        offset = low - base
        other = BLOCK - offset
        rows = []
        for r in range(BLOCK // 8):
            held = rest_ref[low + 8 * r : low + 8 * r + 8, base : base + 128]
            unit = jnp.where(lane == other + 8 * r + sub, 1.0, 0.0)
            rows.append(jnp.where((lane >= offset) & (lane < offset + BLOCK), held, unit))
        block = jnp.concatenate(eliminate(rows, offset, sub), axis=0)
        inverse = block[:, other : other + BLOCK]
        if low:
            out_ref[low:high, 0:low] = dot32(inverse, out_ref[low:high, 0:low], 1, 0)
        out_ref[low:high, low:high] = inverse
        if high < RANK:
            upper = dot32(inverse, rest_ref[low:high, high:RANK], 1, 0)
            solved = out_ref[low:high, 0:high]
            rest_ref[high:RANK, high:RANK] = rest_ref[high:RANK, high:RANK] - dot32(
                upper, upper, 0, 0
            )
            out_ref[high:RANK, 0:high] = out_ref[high:RANK, 0:high] - dot32(upper, solved, 0, 0)


def inverse_factor(gram_matrix):
    return pl.pallas_call(
        inverse_factor_kernel,
        out_shape=jax.ShapeDtypeStruct((RANK, RANK), jnp.float32),
        in_specs=[pl.BlockSpec(memory_space=pltpu.VMEM)],
        out_specs=pl.BlockSpec(memory_space=pltpu.VMEM),
        scratch_shapes=[pltpu.VMEM((RANK, RANK), jnp.float32)],
        cost_estimate=pl.CostEstimate(flops=400_000_000, bytes_accessed=524288, transcendentals=0),
        name="inverse_factor",
    )(gram_matrix)


def scatter_sum(x, axes, count):
    parts = x.reshape(count, x.shape[0] // count, x.shape[1])
    return jnp.sum(lax.all_to_all(parts, axes, 0, 0, tiled=True), axis=0)


def gather(x, axes, count):
    return lax.all_to_all(
        jnp.broadcast_to(x[None], (count,) + x.shape), axes, 0, 0, tiled=True
    )


def project_kernel(near_ref, buffer_ref, left_ref, *refs):
    out_refs, part_ref = refs[:-1], refs[-1]
    left = left_ref[...]
    high = left.astype(jnp.bfloat16)
    rest = left - high.astype(jnp.float32)
    middle = rest.astype(jnp.bfloat16)
    low = (rest - middle.astype(jnp.float32)).astype(jnp.bfloat16)
    own = near_ref[0]
    for i in range(buffer_ref.shape[1] // RANK):
        block = buffer_ref[:, i * RANK : (i + 1) * RANK]
        part_ref[i] = sum(
            lax.dot_general(
                block, piece, (((0,), (0,)), ((), ())), preferred_element_type=jnp.float32
            )
            for piece in (low, middle, high)
        )
        for shift in range(NEAR):
            start = pl.multiple_of(lax.rem(own + shift, NEAR) * SPAN, SPAN)
            out_refs[shift][i * SPAN : (i + 1) * SPAN, :] = part_ref[i, pl.ds(start, SPAN), :]


def project(buffer, left_raw, own):
    columns = buffer.shape[1]
    return pl.pallas_call(
        project_kernel,
        out_shape=[jax.ShapeDtypeStruct((columns // NEAR, RANK), jnp.float32)] * NEAR,
        in_specs=[pl.BlockSpec(memory_space=pltpu.SMEM)]
        + [pl.BlockSpec(memory_space=pltpu.VMEM)] * 2,
        out_specs=[pl.BlockSpec(memory_space=pltpu.VMEM)] * NEAR,
        scratch_shapes=[pltpu.VMEM((columns // RANK, RANK, RANK), jnp.float32)],
        compiler_params=pltpu.CompilerParams(vmem_limit_bytes=32 * 1024 * 1024),
        cost_estimate=pl.CostEstimate(
            flops=6 * buffer.size * RANK, bytes_accessed=3_000_000, transcendentals=0
        ),
        name="project",
    )(own.reshape(1), buffer, left_raw)


def local(wide, tall, momentum, gradient, right_prev):
    place = lax.axis_index(WIDE)
    far = tall // NEAR
    strided = [[i * NEAR + j for i in range(far)] for j in range(NEAR)]
    buffer = (momentum.astype(jnp.float32) + gradient.astype(jnp.float32)).astype(jnp.bfloat16)
    left_partial = jnp.dot(buffer, right_prev, preferred_element_type=jnp.float32)
    rows = left_partial.shape[0]
    left_rows = scatter_sum(left_partial, WIDE, wide)
    left_raw = gather(left_rows, WIDE, wide).reshape(rows, RANK)

    share = RANK // wide
    own = lax.dynamic_slice(left_raw, (0, place * share), (rows, share))
    gram_rows = jnp.sum(gather(dot32(own, left_raw, 0, 0), "row", tall), axis=0)
    blocks = list(project(buffer, left_raw, lax.rem(lax.axis_index("row"), NEAR)))

    for shift in range(1, NEAR):
        ring = [(i, i // NEAR * NEAR + (i + shift) % NEAR) for i in range(tall)]
        blocks[shift] = lax.ppermute(blocks[shift], "row", ring)
    gram_matrix = gather(gram_rows, WIDE, wide).reshape(RANK, RANK)
    blocks = sum(blocks).reshape(far, SPAN, RANK)

    gram_matrix, blocks = lax.optimization_barrier((gram_matrix, blocks))
    blocks = lax.all_to_all(blocks, "row", 0, 0, axis_index_groups=strided, tiled=True)
    inverse = inverse_factor(gram_matrix)
    right_raw = jnp.sum(blocks, axis=0)

    left_factor = dot32(left_raw, inverse, 1, 1)
    left_low = left_factor.astype(jnp.bfloat16)
    right_rows = dot32(right_raw, inverse, 1, 1).astype(jnp.bfloat16)
    right_low = lax.all_gather(right_rows, "row", axis=0, tiled=True)
    right_wide = right_low.astype(jnp.float32)
    own_sums = jnp.sum(right_wide * right_wide, axis=0, keepdims=True)
    column_sums = jnp.sum(gather(own_sums, WIDE, wide), axis=0)
    outer = lax.dot_general(
        left_low, right_low, (((1,), (1,)), ((), ())), preferred_element_type=jnp.float32
    )
    momentum_next = (buffer.astype(jnp.float32) - 0.1 * outer).astype(jnp.bfloat16)
    right_factor = right_wide / (jnp.sqrt(column_sums) + 1e-08)
    return (momentum_next, left_factor, right_factor)


def solution(mesh):
    wide = mesh.shape["col"] * mesh.shape["rep"]
    tall = mesh.shape["row"]
    placed = (P("row", WIDE), P("row", WIDE), P(WIDE, None))

    def run(momentum, gradient, right_prev):
        return local(wide, tall, momentum, gradient, right_prev)

    return jax.shard_map(
        run,
        mesh=mesh,
        in_specs=placed,
        out_specs=(P("row", WIDE), P("row", None), P(WIDE, None)),
        check_vma=False,
    )
```

```python
import jax
import jax.numpy as jnp
from jax import lax
from jax.experimental import pallas as pl
from jax.experimental.pallas import tpu as pltpu
from jax.sharding import PartitionSpec as P

RANK = 256
BLOCK = 64
SPAN = 64
NEAR = 4
WIDE = ("col", "rep")


def dot32(a, b, a_dim, b_dim):
    return lax.dot_general(
        a,
        b,
        (((a_dim,), (b_dim,)), ((), ())),
        precision=lax.Precision.HIGHEST,
        preferred_element_type=jnp.float32,
    )


def eliminate(rows, offset, sub):
    count = len(rows)
    done = []
    for group in range(count):
        first = offset + 8 * group
        cols = [
            [
                jnp.broadcast_to(rows[r][:, first + k : first + k + 1], (8, 128))
                for k in range(8)
            ]
            for r in range(group, count)
        ]
        scale = jnp.zeros((8, 128), jnp.float32)
        for k in range(8):
            pivot = jnp.broadcast_to(cols[0][k][k : k + 1, :], (8, 128))
            inverse = 1.0 / pivot
            scale = jnp.where(sub == k, lax.rsqrt(pivot), scale)
            pivot_row = jnp.broadcast_to(rows[group][k : k + 1, :], (8, 128)) * inverse
            pivot_cols = [
                jnp.broadcast_to(cols[0][j][k : k + 1, :], (8, 128)) * inverse
                for j in range(k + 1, 8)
            ]
            for r in range(group, count):
                factor = cols[r - group][k]
                if r == group:
                    if k == 7:
                        continue
                    factor = jnp.where(sub > k, factor, 0.0)
                rows[r] = rows[r] - factor * pivot_row
                for j in range(k + 1, 8):
                    cols[r - group][j] = cols[r - group][j] - factor * pivot_cols[j - k - 1]
        done.append(rows[group] * scale)
    return done


def inverse_factor_kernel(gram_ref, out_ref, rest_ref):
    sub = lax.broadcasted_iota(jnp.int32, (8, 128), 0)
    lane = lax.broadcasted_iota(jnp.int32, (8, 128), 1)
    rest_ref[...] = gram_ref[...]
    out_ref[...] = jnp.zeros((RANK, RANK), jnp.float32)
    for low in range(0, RANK, BLOCK):
        high = low + BLOCK
        base = low // 128 * 128
        offset = low - base
        other = BLOCK - offset
        rows = []
        for r in range(BLOCK // 8):
            held = rest_ref[low + 8 * r : low + 8 * r + 8, base : base + 128]
            unit = jnp.where(lane == other + 8 * r + sub, 1.0, 0.0)
            rows.append(jnp.where((lane >= offset) & (lane < offset + BLOCK), held, unit))
        block = jnp.concatenate(eliminate(rows, offset, sub), axis=0)
        inverse = block[:, other : other + BLOCK]
        if low:
            out_ref[low:high, 0:low] = dot32(inverse, out_ref[low:high, 0:low], 1, 0)
        out_ref[low:high, low:high] = inverse
        if high < RANK:
            upper = dot32(inverse, rest_ref[low:high, high:RANK], 1, 0)
            solved = out_ref[low:high, 0:high]
            rest_ref[high:RANK, high:RANK] = rest_ref[high:RANK, high:RANK] - dot32(
                upper, upper, 0, 0
            )
            out_ref[high:RANK, 0:high] = out_ref[high:RANK, 0:high] - dot32(upper, solved, 0, 0)


def inverse_factor(gram_matrix):
    return pl.pallas_call(
        inverse_factor_kernel,
        out_shape=jax.ShapeDtypeStruct((RANK, RANK), jnp.float32),
        in_specs=[pl.BlockSpec(memory_space=pltpu.VMEM)],
        out_specs=pl.BlockSpec(memory_space=pltpu.VMEM),
        scratch_shapes=[pltpu.VMEM((RANK, RANK), jnp.float32)],
        cost_estimate=pl.CostEstimate(flops=400_000_000, bytes_accessed=524288, transcendentals=0),
        name="inverse_factor",
    )(gram_matrix)


def accumulate_kernel(momentum_ref, gradient_ref, right_ref, buffer_ref, left_ref, *scratch):
    momentum, gradient, right, sems = scratch
    count = sems.shape[0] - 1
    rows = momentum.shape[0] // count
    fetch_right = pltpu.make_async_copy(right_ref, right, sems.at[count, 0])
    fetches = []
    for i in range(count):
        part = pl.ds(i * rows, rows)
        fetches.append(
            [
                pltpu.make_async_copy(source.at[part], target.at[part], sems.at[i, j])
                for j, (source, target) in enumerate(
                    [(momentum_ref, momentum), (gradient_ref, gradient)]
                )
            ]
        )
    for fetch in fetches[0]:
        fetch.start()
    fetch_right.start()
    for pair in fetches[1:]:
        for fetch in pair:
            fetch.start()
    for i in range(count):
        part = slice(i * rows, (i + 1) * rows)
        for fetch in fetches[i]:
            fetch.wait()
        total = momentum[part, :].astype(jnp.float32) + gradient[part, :].astype(jnp.float32)
        total = total.astype(jnp.bfloat16)
        buffer_ref[part, :] = total
        if i == 0:
            fetch_right.wait()
        left_ref[part, :] = jnp.dot(total, right[...], preferred_element_type=jnp.float32)


def accumulate(momentum, gradient, right_prev):
    rows, columns = momentum.shape
    chunks = 4
    return pl.pallas_call(
        accumulate_kernel,
        out_shape=[
            jax.ShapeDtypeStruct((rows, columns), jnp.bfloat16),
            jax.ShapeDtypeStruct((rows, RANK), jnp.float32),
        ],
        in_specs=[pl.BlockSpec(memory_space=pl.ANY)] * 3,
        out_specs=[pl.BlockSpec(memory_space=pltpu.VMEM)] * 2,
        scratch_shapes=[
            pltpu.VMEM((rows, columns), jnp.bfloat16),
            pltpu.VMEM((rows, columns), jnp.bfloat16),
            pltpu.VMEM((columns, RANK), jnp.bfloat16),
            pltpu.SemaphoreType.DMA((chunks + 1, 2)),
        ],
        cost_estimate=pl.CostEstimate(
            flops=2 * rows * columns * RANK, bytes_accessed=4_000_000, transcendentals=0
        ),
        name="accumulate",
    )(momentum, gradient, right_prev)


def scatter_sum(x, axes, count):
    parts = x.reshape(count, x.shape[0] // count, x.shape[1])
    return jnp.sum(lax.all_to_all(parts, axes, 0, 0, tiled=True), axis=0)


def gather(x, axes, count):
    return lax.all_to_all(
        jnp.broadcast_to(x[None], (count,) + x.shape), axes, 0, 0, tiled=True
    )


def project_kernel(near_ref, buffer_ref, left_ref, *refs):
    out_refs, part_ref = refs[:-1], refs[-1]
    left = left_ref[...]
    high = left.astype(jnp.bfloat16)
    rest = left - high.astype(jnp.float32)
    middle = rest.astype(jnp.bfloat16)
    low = (rest - middle.astype(jnp.float32)).astype(jnp.bfloat16)
    own = near_ref[0]
    for i in range(buffer_ref.shape[1] // RANK):
        block = buffer_ref[:, i * RANK : (i + 1) * RANK]
        part_ref[i] = sum(
            lax.dot_general(
                block, piece, (((0,), (0,)), ((), ())), preferred_element_type=jnp.float32
            )
            for piece in (low, middle, high)
        )
        for shift in range(NEAR):
            start = pl.multiple_of(lax.rem(own + shift, NEAR) * SPAN, SPAN)
            out_refs[shift][i * SPAN : (i + 1) * SPAN, :] = part_ref[i, pl.ds(start, SPAN), :]


def project(buffer, left_raw, own):
    columns = buffer.shape[1]
    return pl.pallas_call(
        project_kernel,
        out_shape=[jax.ShapeDtypeStruct((columns // NEAR, RANK), jnp.float32)] * NEAR,
        in_specs=[pl.BlockSpec(memory_space=pltpu.SMEM)]
        + [pl.BlockSpec(memory_space=pltpu.VMEM)] * 2,
        out_specs=[pl.BlockSpec(memory_space=pltpu.VMEM)] * NEAR,
        scratch_shapes=[pltpu.VMEM((columns // RANK, RANK, RANK), jnp.float32)],
        compiler_params=pltpu.CompilerParams(vmem_limit_bytes=32 * 1024 * 1024),
        cost_estimate=pl.CostEstimate(
            flops=6 * buffer.size * RANK, bytes_accessed=3_000_000, transcendentals=0
        ),
        name="project",
    )(own.reshape(1), buffer, left_raw)


def finish_kernel(left_ref, inverse_ref, right_ref, buffer_ref, factor_ref, next_ref):
    factor = dot32(left_ref[...], inverse_ref[...], 1, 1)
    factor_ref[...] = factor
    outer = lax.dot_general(
        factor.astype(jnp.bfloat16),
        right_ref[...],
        (((1,), (1,)), ((), ())),
        preferred_element_type=jnp.float32,
    )
    next_ref[...] = (buffer_ref[...].astype(jnp.float32) - 0.1 * outer).astype(jnp.bfloat16)


def finish(left_raw, inverse, right_low, buffer):
    rows, columns = buffer.shape
    tile = rows // 4
    return pl.pallas_call(
        finish_kernel,
        out_shape=[
            jax.ShapeDtypeStruct((rows, RANK), jnp.float32),
            jax.ShapeDtypeStruct((rows, columns), jnp.bfloat16),
        ],
        grid=(rows // tile,),
        in_specs=[
            pl.BlockSpec((tile, RANK), lambda i: (i, 0)),
            pl.BlockSpec((RANK, RANK), lambda i: (0, 0)),
            pl.BlockSpec((columns, RANK), lambda i: (0, 0)),
            pl.BlockSpec((tile, columns), lambda i: (i, 0)),
        ],
        out_specs=[
            pl.BlockSpec((tile, RANK), lambda i: (i, 0)),
            pl.BlockSpec((tile, columns), lambda i: (i, 0)),
        ],
        cost_estimate=pl.CostEstimate(
            flops=2 * rows * columns * RANK, bytes_accessed=4_000_000, transcendentals=0
        ),
        name="finish",
    )(left_raw, inverse, right_low, buffer)


def local(wide, tall, momentum, gradient, right_prev):
    place = lax.axis_index(WIDE)
    far = tall // NEAR
    strided = [[i * NEAR + j for i in range(far)] for j in range(NEAR)]
    buffer, left_partial = accumulate(momentum, gradient, right_prev)
    rows = left_partial.shape[0]
    left_rows = scatter_sum(left_partial, WIDE, wide)
    left_raw = gather(left_rows, WIDE, wide).reshape(rows, RANK)

    share = RANK // wide
    own = lax.dynamic_slice(left_raw, (0, place * share), (rows, share))
    gram_rows = jnp.sum(gather(dot32(own, left_raw, 0, 0), "row", tall), axis=0)
    blocks = list(project(buffer, left_raw, lax.rem(lax.axis_index("row"), NEAR)))

    for shift in range(1, NEAR):
        ring = [(i, i // NEAR * NEAR + (i + shift) % NEAR) for i in range(tall)]
        blocks[shift] = lax.ppermute(blocks[shift], "row", ring)
    gram_matrix = gather(gram_rows, WIDE, wide).reshape(RANK, RANK)
    early = lax.optimization_barrier(sum(blocks[:-1]))
    blocks = (early + blocks[-1]).reshape(far, SPAN, RANK)

    gram_matrix, blocks = lax.optimization_barrier((gram_matrix, blocks))
    blocks = lax.all_to_all(blocks, "row", 0, 0, axis_index_groups=strided, tiled=True)
    inverse = inverse_factor(gram_matrix)
    right_raw = jnp.sum(blocks, axis=0)

    right_rows = dot32(right_raw, inverse, 1, 1).astype(jnp.bfloat16)
    right_low = lax.all_gather(right_rows, "row", axis=0, tiled=True)
    right_wide = right_low.astype(jnp.float32)
    own_sums = jnp.sum(right_wide * right_wide, axis=0, keepdims=True)
    column_sums = jnp.sum(gather(own_sums, WIDE, wide), axis=0)
    left_factor, momentum_next = finish(left_raw, inverse, right_low, buffer)
    right_factor = right_wide / (jnp.sqrt(column_sums) + 1e-08)
    return (momentum_next, left_factor, right_factor)


def solution(mesh):
    wide = mesh.shape["col"] * mesh.shape["rep"]
    tall = mesh.shape["row"]
    placed = (P("row", WIDE), P("row", WIDE), P(WIDE, None))

    def run(momentum, gradient, right_prev):
        return local(wide, tall, momentum, gradient, right_prev)

    return jax.shard_map(
        run,
        mesh=mesh,
        in_specs=placed,
        out_specs=(P("row", WIDE), P("row", None), P(WIDE, None)),
        check_vma=False,
    )
```

```python
import jax
import jax.numpy as jnp
from jax import lax
from jax.experimental import pallas as pl
from jax.experimental.pallas import tpu as pltpu
from jax.sharding import PartitionSpec as P

RANK = 256
BLOCK = 64
NEAR = 4
WIDE = ("col", "rep")


def dot32(a, b, a_dim, b_dim):
    return lax.dot_general(
        a,
        b,
        (((a_dim,), (b_dim,)), ((), ())),
        precision=lax.Precision.HIGHEST,
        preferred_element_type=jnp.float32,
    )


def eliminate(rows, offset, sub):
    count = len(rows)
    done = []
    for group in range(count):
        first = offset + 8 * group
        cols = [
            [
                jnp.broadcast_to(rows[r][:, first + k : first + k + 1], (8, 128))
                for k in range(8)
            ]
            for r in range(group, count)
        ]
        scale = jnp.zeros((8, 128), jnp.float32)
        for k in range(8):
            pivot = jnp.broadcast_to(cols[0][k][k : k + 1, :], (8, 128))
            inverse = 1.0 / pivot
            scale = jnp.where(sub == k, lax.rsqrt(pivot), scale)
            pivot_row = jnp.broadcast_to(rows[group][k : k + 1, :], (8, 128)) * inverse
            pivot_cols = [
                jnp.broadcast_to(cols[0][j][k : k + 1, :], (8, 128)) * inverse
                for j in range(k + 1, 8)
            ]
            for r in range(group, count):
                factor = cols[r - group][k]
                if r == group:
                    if k == 7:
                        continue
                    factor = jnp.where(sub > k, factor, 0.0)
                rows[r] = rows[r] - factor * pivot_row
                for j in range(k + 1, 8):
                    cols[r - group][j] = cols[r - group][j] - factor * pivot_cols[j - k - 1]
        done.append(rows[group] * scale)
    return done


def factor_kernel(gram_ref, left_ref, total_ref, factor_ref, part_ref, rest_ref, inv_ref):
    sub = lax.broadcasted_iota(jnp.int32, (8, 128), 0)
    lane = lax.broadcasted_iota(jnp.int32, (8, 128), 1)
    rest_ref[...] = gram_ref[...]
    inv_ref[...] = jnp.zeros((RANK, RANK), jnp.float32)
    held = gram_ref[0:BLOCK, 0:128]
    for low in range(0, RANK, BLOCK):
        high = low + BLOCK
        offset = low % 128
        other = BLOCK - offset
        rows = []
        for r in range(BLOCK // 8):
            unit = jnp.where(lane == other + 8 * r + sub, 1.0, 0.0)
            inside = (lane >= offset) & (lane < offset + BLOCK)
            rows.append(jnp.where(inside, held[8 * r : 8 * r + 8, :], unit))
        block = jnp.concatenate(eliminate(rows, offset, sub), axis=0)
        inverse = block[:, other : other + BLOCK]
        if high < RANK:
            base = high // 128 * 128
            near = dot32(inverse, rest_ref[low:high, base : base + 128], 1, 0)
            held = rest_ref[high : high + BLOCK, base : base + 128] - dot32(
                near[:, high - base : high - base + BLOCK], near, 0, 0
            )
        if low:
            inv_ref[low:high, 0:low] = dot32(inverse, inv_ref[low:high, 0:low], 1, 0)
        inv_ref[low:high, low:high] = inverse
        if high < RANK:
            upper = dot32(inverse, rest_ref[low:high, high:RANK], 1, 0)
            solved = inv_ref[low:high, 0:high]
            rest_ref[high:RANK, high:RANK] = rest_ref[high:RANK, high:RANK] - dot32(
                upper, upper, 0, 0
            )
            inv_ref[high:RANK, 0:high] = inv_ref[high:RANK, 0:high] - dot32(upper, solved, 0, 0)
    part_ref[...] = dot32(total_ref[...], inv_ref[...], 1, 1).astype(jnp.bfloat16)
    factor_ref[...] = dot32(left_ref[...], inv_ref[...], 1, 1)


def apply_factor(gram_matrix, left_raw, total):
    return pl.pallas_call(
        factor_kernel,
        out_shape=[
            jax.ShapeDtypeStruct(left_raw.shape, jnp.float32),
            jax.ShapeDtypeStruct(total.shape, jnp.bfloat16),
        ],
        in_specs=[pl.BlockSpec(memory_space=pltpu.VMEM)] * 3,
        out_specs=[pl.BlockSpec(memory_space=pltpu.VMEM)] * 2,
        scratch_shapes=[pltpu.VMEM((RANK, RANK), jnp.float32)] * 2,
        compiler_params=pltpu.CompilerParams(vmem_limit_bytes=32 * 1024 * 1024),
        cost_estimate=pl.CostEstimate(flops=600_000_000, bytes_accessed=2_000_000, transcendentals=0),
        name="apply_factor",
    )(gram_matrix, left_raw, total)


def scatter_sum(x, axes, count):
    parts = x.reshape(count, x.shape[0] // count, x.shape[1])
    return jnp.sum(lax.all_to_all(parts, axes, 0, 0, tiled=True), axis=0)


def gather(x, axes, count):
    return lax.all_to_all(
        jnp.broadcast_to(x[None], (count,) + x.shape), axes, 0, 0, tiled=True
    )


def project_kernel(near_ref, buffer_ref, left_ref, *out_refs):
    left = left_ref[...]
    high = left.astype(jnp.bfloat16)
    rest = left - high.astype(jnp.float32)
    middle = rest.astype(jnp.bfloat16)
    low = (rest - middle.astype(jnp.float32)).astype(jnp.bfloat16)
    count = len(out_refs)
    span = buffer_ref.shape[1] // count
    for shift in range(count):
        start = pl.multiple_of(lax.rem(near_ref[0] + shift, count) * span, span)
        block = buffer_ref[:, pl.ds(start, span)]
        out_refs[shift][...] = sum(
            lax.dot_general(
                block, piece, (((0,), (0,)), ((), ())), preferred_element_type=jnp.float32
            )
            for piece in (low, middle, high)
        )


def project(buffer, left_raw, own):
    columns = buffer.shape[1]
    return pl.pallas_call(
        project_kernel,
        out_shape=[jax.ShapeDtypeStruct((columns // NEAR, RANK), jnp.float32)] * NEAR,
        in_specs=[pl.BlockSpec(memory_space=pltpu.SMEM)]
        + [pl.BlockSpec(memory_space=pltpu.VMEM)] * 2,
        out_specs=[pl.BlockSpec(memory_space=pltpu.VMEM)] * NEAR,
        compiler_params=pltpu.CompilerParams(vmem_limit_bytes=32 * 1024 * 1024),
        cost_estimate=pl.CostEstimate(
            flops=6 * buffer.size * RANK, bytes_accessed=3_000_000, transcendentals=0
        ),
        name="project",
    )(own.reshape(1), buffer, left_raw)


def local(wide, tall, momentum, gradient, right_prev):
    place = lax.axis_index(WIDE)
    far = tall // NEAR
    adjacent = [[i * NEAR + j for j in range(NEAR)] for i in range(far)]
    strided = [[i * NEAR + j for i in range(far)] for j in range(NEAR)]
    buffer = (momentum.astype(jnp.float32) + gradient.astype(jnp.float32)).astype(jnp.bfloat16)
    left_partial = jnp.dot(buffer, right_prev, preferred_element_type=jnp.float32)
    rows = left_partial.shape[0]
    left_rows = scatter_sum(left_partial, WIDE, wide)
    left_raw = gather(left_rows, WIDE, wide).reshape(rows, RANK)

    share = RANK // wide
    own = lax.dynamic_slice(left_raw, (0, place * share), (rows, share))
    gram_rows = jnp.sum(gather(dot32(own, left_raw, 0, 0), "row", tall), axis=0)
    blocks = list(project(buffer, left_raw, lax.rem(lax.axis_index("row"), NEAR)))

    gram_matrix = gather(gram_rows, WIDE, wide).reshape(RANK, RANK)
    for shift in range(1, NEAR):
        ring = [(i, i // NEAR * NEAR + (i + shift) % NEAR) for i in range(tall)]
        blocks[shift] = lax.ppermute(blocks[shift], "row", ring)
    gram_matrix, total = lax.optimization_barrier((gram_matrix, sum(blocks)))
    left_factor, part = apply_factor(gram_matrix, left_raw, total)
    left_low = left_factor.astype(jnp.bfloat16)
    parts = lax.all_gather(part, "row", axis=0, axis_index_groups=strided)
    right_rows = jnp.sum(parts.astype(jnp.float32), axis=0).astype(jnp.bfloat16)
    right_low = lax.all_gather(
        right_rows, "row", axis=0, axis_index_groups=adjacent, tiled=True
    )
    right_wide = right_low.astype(jnp.float32)
    own_sums = jnp.sum(right_wide * right_wide, axis=0, keepdims=True)
    column_sums = jnp.sum(gather(own_sums, WIDE, wide), axis=0)
    outer = lax.dot_general(
        left_low, right_low, (((1,), (1,)), ((), ())), preferred_element_type=jnp.float32
    )
    momentum_next = (buffer.astype(jnp.float32) - 0.1 * outer).astype(jnp.bfloat16)
    right_factor = right_wide / (jnp.sqrt(column_sums) + 1e-08)
    return (momentum_next, left_factor, right_factor)


def solution(mesh):
    wide = mesh.shape["col"] * mesh.shape["rep"]
    tall = mesh.shape["row"]
    placed = (P("row", WIDE), P("row", WIDE), P(WIDE, None))

    def run(momentum, gradient, right_prev):
        return local(wide, tall, momentum, gradient, right_prev)

    return jax.shard_map(
        run,
        mesh=mesh,
        in_specs=placed,
        out_specs=(P("row", WIDE), P("row", None), P(WIDE, None)),
        check_vma=False,
    )
```

```python
import jax
import jax.numpy as jnp
from jax import lax
from jax.experimental import pallas as pl
from jax.experimental.pallas import tpu as pltpu
from jax.sharding import PartitionSpec as P

RANK = 256
BLOCK = 64
NEAR = 4
WIDE = ("col", "rep")


def dot32(a, b, a_dim, b_dim):
    return lax.dot_general(
        a,
        b,
        (((a_dim,), (b_dim,)), ((), ())),
        precision=lax.Precision.HIGHEST,
        preferred_element_type=jnp.float32,
    )


def eliminate(rows, offset, sub):
    count = len(rows)
    done = []
    for group in range(count):
        first = offset + 8 * group
        cols = [
            [
                jnp.broadcast_to(rows[r][:, first + k : first + k + 1], (8, 128))
                for k in range(8)
            ]
            for r in range(group, count)
        ]
        scale = jnp.zeros((8, 128), jnp.float32)
        for k in range(8):
            pivot = jnp.broadcast_to(cols[0][k][k : k + 1, :], (8, 128))
            inverse = 1.0 / pivot
            scale = jnp.where(sub == k, lax.rsqrt(pivot), scale)
            pivot_row = jnp.broadcast_to(rows[group][k : k + 1, :], (8, 128)) * inverse
            pivot_cols = [
                jnp.broadcast_to(cols[0][j][k : k + 1, :], (8, 128)) * inverse
                for j in range(k + 1, 8)
            ]
            for r in range(group, count):
                factor = cols[r - group][k]
                if r == group:
                    if k == 7:
                        continue
                    factor = jnp.where(sub > k, factor, 0.0)
                rows[r] = rows[r] - factor * pivot_row
                for j in range(k + 1, 8):
                    cols[r - group][j] = cols[r - group][j] - factor * pivot_cols[j - k - 1]
        done.append(rows[group] * scale)
    return done


def factor_kernel(gram_ref, left_ref, factor_ref, inv_ref, rest_ref):
    sub = lax.broadcasted_iota(jnp.int32, (8, 128), 0)
    lane = lax.broadcasted_iota(jnp.int32, (8, 128), 1)
    rest_ref[...] = gram_ref[...]
    inv_ref[...] = jnp.zeros((RANK, RANK), jnp.float32)
    held = gram_ref[0:BLOCK, 0:128]
    for low in range(0, RANK, BLOCK):
        high = low + BLOCK
        offset = low % 128
        other = BLOCK - offset
        rows = []
        for r in range(BLOCK // 8):
            unit = jnp.where(lane == other + 8 * r + sub, 1.0, 0.0)
            inside = (lane >= offset) & (lane < offset + BLOCK)
            rows.append(jnp.where(inside, held[8 * r : 8 * r + 8, :], unit))
        block = jnp.concatenate(eliminate(rows, offset, sub), axis=0)
        inverse = block[:, other : other + BLOCK]
        if high < RANK:
            base = high // 128 * 128
            near = dot32(inverse, rest_ref[low:high, base : base + 128], 1, 0)
            held = rest_ref[high : high + BLOCK, base : base + 128] - dot32(
                near[:, high - base : high - base + BLOCK], near, 0, 0
            )
        if low:
            inv_ref[low:high, 0:low] = dot32(inverse, inv_ref[low:high, 0:low], 1, 0)
        inv_ref[low:high, low:high] = inverse
        if high < RANK:
            upper = dot32(inverse, rest_ref[low:high, high:RANK], 1, 0)
            solved = inv_ref[low:high, 0:high]
            rest_ref[high:RANK, high:RANK] = rest_ref[high:RANK, high:RANK] - dot32(
                upper, upper, 0, 0
            )
            inv_ref[high:RANK, 0:high] = inv_ref[high:RANK, 0:high] - dot32(upper, solved, 0, 0)
    factor_ref[...] = dot32(left_ref[...], inv_ref[...], 1, 1)


def apply_factor(gram_matrix, left_raw):
    return pl.pallas_call(
        factor_kernel,
        out_shape=[
            jax.ShapeDtypeStruct(left_raw.shape, jnp.float32),
            jax.ShapeDtypeStruct((RANK, RANK), jnp.float32),
        ],
        in_specs=[pl.BlockSpec(memory_space=pltpu.VMEM)] * 2,
        out_specs=[pl.BlockSpec(memory_space=pltpu.VMEM)] * 2,
        scratch_shapes=[pltpu.VMEM((RANK, RANK), jnp.float32)],
        compiler_params=pltpu.CompilerParams(vmem_limit_bytes=32 * 1024 * 1024),
        cost_estimate=pl.CostEstimate(flops=600_000_000, bytes_accessed=2_000_000, transcendentals=0),
        name="apply_factor",
    )(gram_matrix, left_raw)


def scatter_sum(x, axes, count):
    parts = x.reshape(count, x.shape[0] // count, x.shape[1])
    return jnp.sum(lax.all_to_all(parts, axes, 0, 0, tiled=True), axis=0)


def gather(x, axes, count):
    return lax.all_to_all(
        jnp.broadcast_to(x[None], (count,) + x.shape), axes, 0, 0, tiled=True
    )


def project_kernel(near_ref, buffer_ref, left_ref, *out_refs):
    left = left_ref[...]
    high = left.astype(jnp.bfloat16)
    rest = left - high.astype(jnp.float32)
    middle = rest.astype(jnp.bfloat16)
    low = (rest - middle.astype(jnp.float32)).astype(jnp.bfloat16)
    count = len(out_refs)
    span = buffer_ref.shape[1] // count
    for shift in range(count):
        start = pl.multiple_of(lax.rem(near_ref[0] + shift, count) * span, span)
        block = buffer_ref[:, pl.ds(start, span)]
        out_refs[shift][...] = sum(
            lax.dot_general(
                block, piece, (((0,), (0,)), ((), ())), preferred_element_type=jnp.float32
            )
            for piece in (low, middle, high)
        )


def project(buffer, left_raw, own):
    columns = buffer.shape[1]
    return pl.pallas_call(
        project_kernel,
        out_shape=[jax.ShapeDtypeStruct((columns // NEAR, RANK), jnp.float32)] * NEAR,
        in_specs=[pl.BlockSpec(memory_space=pltpu.SMEM)]
        + [pl.BlockSpec(memory_space=pltpu.VMEM)] * 2,
        out_specs=[pl.BlockSpec(memory_space=pltpu.VMEM)] * NEAR,
        compiler_params=pltpu.CompilerParams(vmem_limit_bytes=32 * 1024 * 1024),
        cost_estimate=pl.CostEstimate(
            flops=6 * buffer.size * RANK, bytes_accessed=3_000_000, transcendentals=0
        ),
        name="project",
    )(own.reshape(1), buffer, left_raw)


def local(wide, tall, momentum, gradient, right_prev):
    place = lax.axis_index(WIDE)
    far = tall // NEAR
    adjacent = [[i * NEAR + j for j in range(NEAR)] for i in range(far)]
    strided = [[i * NEAR + j for i in range(far)] for j in range(NEAR)]
    buffer = (momentum.astype(jnp.float32) + gradient.astype(jnp.float32)).astype(jnp.bfloat16)
    left_partial = jnp.dot(buffer, right_prev, preferred_element_type=jnp.float32)
    rows = left_partial.shape[0]
    left_rows = scatter_sum(left_partial, WIDE, wide)
    left_raw = gather(left_rows, WIDE, wide).reshape(rows, RANK)

    share = RANK // wide
    own = lax.dynamic_slice(left_raw, (0, place * share), (rows, share))
    gram_rows = jnp.sum(gather(dot32(own, left_raw, 0, 0), "row", tall), axis=0)
    blocks = list(project(buffer, left_raw, lax.rem(lax.axis_index("row"), NEAR)))

    gram_matrix = gather(gram_rows, WIDE, wide).reshape(RANK, RANK)
    for shift in range(1, NEAR):
        ring = [(i, i // NEAR * NEAR + (i + shift) % NEAR) for i in range(tall)]
        blocks[shift] = lax.ppermute(blocks[shift], "row", ring)
    gram_matrix, early = lax.optimization_barrier((gram_matrix, sum(blocks[:-1])))
    left_factor, inverse = apply_factor(gram_matrix, left_raw)
    left_low = left_factor.astype(jnp.bfloat16)
    part = dot32(early + blocks[-1], inverse, 1, 1).astype(jnp.bfloat16)
    parts = lax.all_gather(part, "row", axis=0, axis_index_groups=strided)
    right_rows = jnp.sum(parts.astype(jnp.float32), axis=0).astype(jnp.bfloat16)
    right_low = lax.all_gather(
        right_rows, "row", axis=0, axis_index_groups=adjacent, tiled=True
    )
    right_wide = right_low.astype(jnp.float32)
    own_sums = jnp.sum(right_wide * right_wide, axis=0, keepdims=True)
    column_sums = jnp.sum(gather(own_sums, WIDE, wide), axis=0)
    outer = lax.dot_general(
        left_low, right_low, (((1,), (1,)), ((), ())), preferred_element_type=jnp.float32
    )
    momentum_next = (buffer.astype(jnp.float32) - 0.1 * outer).astype(jnp.bfloat16)
    right_factor = right_wide / (jnp.sqrt(column_sums) + 1e-08)
    return (momentum_next, left_factor, right_factor)


def solution(mesh):
    wide = mesh.shape["col"] * mesh.shape["rep"]
    tall = mesh.shape["row"]
    placed = (P("row", WIDE), P("row", WIDE), P(WIDE, None))

    def run(momentum, gradient, right_prev):
        return local(wide, tall, momentum, gradient, right_prev)

    return jax.shard_map(
        run,
        mesh=mesh,
        in_specs=placed,
        out_specs=(P("row", WIDE), P("row", None), P(WIDE, None)),
        check_vma=False,
    )
```
